32 devices in a mesh: groups: 2 (over y), adapter: 4 (over x, core), tensor: 4 (over z).
Axes of the slice: x: 2, y: 2, z: 4, core: 2. Of those that a mesh axis runs over, the one named last changes fastest.
Arguments:
- normed_hidden: bfloat16 [4096, 4096], P(('groups', 'adapter'), 'tensor'), parts along dimension 0, may hold values from -60 to 60
- query_weight: bfloat16 [4096, 4096], P(None, 'tensor'), may hold values from -0.09375 to 0.09375
- key_value_weight: bfloat16 [2, 4096, 1024], P(None, None, 'tensor'), may hold values from -0.09375 to 0.09375
- output_weight: bfloat16 [4096, 4096], P('tensor'), may hold values from -0.09375 to 0.09375
- adapter_down_rows: bfloat16 [128, 48, 4096], P(('groups', 'adapter')), parts along dimension 0, may hold values from -0.09375 to 0.09375
- adapter_query_up: bfloat16 [128, 16, 4096], P(('groups', 'adapter'), None, 'tensor'), parts along dimension 0, may hold values from -1.5 to 1.5
- adapter_key_value_up: bfloat16 [128, 2, 16, 1024], P(('groups', 'adapter'), None, None, 'tensor'), parts along dimension 0, may hold values from -1.5 to 1.5
- adapter_output_down: bfloat16 [128, 16, 4096], P(('groups', 'adapter'), None, 'tensor'), parts along dimension 0, may hold values from -0.09375 to 0.09375
- adapter_output_up: bfloat16 [128, 16, 4096], P(('groups', 'adapter'), None, 'tensor'), parts along dimension 0, may hold values from -1.5 to 1.5
- adapter_cache_row: int32 [128], P('groups'), parts along dimension 0, may hold values from 0 to 63, as said below
- request_adapter_index: int32 [8, 4], P(('groups', 'adapter')), parts along dimension 0, may hold values from 0 to 63, as said below
- request_token_length: int32 [8, 4], P(('groups', 'adapter')), parts along dimension 0, may hold values from 1 to 256, 512 in all within a row
Outputs:
- mixed: bfloat16 [4096, 4096], P(('groups', 'adapter'), 'tensor'), parts along dimension 0
- kv_cache: bfloat16 [2, 4096, 1024], P(None, ('groups', 'adapter'), 'tensor'), parts along dimension 1
The draws below stay inside these ranges and needn't reach their ends.
There are 2 independent parts, one for each index of `groups`. The reference program is written for one: setup_inputs(seed, part) draws one part's arguments, and reference() takes and returns one part's arrays. A program takes and returns all parts, laid end to end along the dimension named above; an argument that names none is the same for every part. Nothing has to cross between parts.
Inputs may be any that keep to these rules, and one draw needn't show every extreme that they name: `adapter_cache_row`: a permutation of the cache rows. `request_adapter_index`: in each row, at most 2 requests name adapters whose adapter_cache_row values lie in one aligned block of 16 values, and in every row some block holds exactly 2. `request_token_length`: each row sums to 512.
All inputs are finite; a program needn't handle non-finite values.
Results may differ from the reference program's by a relative error of at most 0.012.
The reference program's roundings to bfloat16 on the way (of `low_in`, `weights`, `attended` and `low_out`) count: a program that leaves them out, or rounds other values in their place, can miss the bound.
Values may be sent and summed in bfloat16 or wider, within the bound.
A program may use at most 128 MiB of HBM per device.

```python
import math
import jax
import jax.numpy as jnp
import numpy as np
from jax import lax

MODEL_WIDTH = 4096
QUERY_HEADS = 32
KEY_VALUE_HEADS = 8
HEAD_WIDTH = 128
ADAPTER_RANK = 16
ADAPTER_COUNT = 64
CAP = 2
TOKENS_PER_ROW = 512
REQUESTS_PER_ROW = 4
TOKEN_TOTAL = 2048
N_ADAPTER = 4


def adapter_layout(key):
    home_key, run_key = jax.random.split(jax.random.fold_in(key, 7))
    home_table = jax.random.permutation(home_key, ADAPTER_COUNT).astype(jnp.int32)
    inverse = jnp.argsort(home_table).astype(jnp.int32)
    held_adapter_count = ADAPTER_COUNT // N_ADAPTER

    def one_run(single_key):
        top_key, rest_key, slot_key, order_key = jax.random.split(single_key, 4)
        busiest = jax.random.randint(top_key, (), 0, N_ADAPTER).astype(jnp.int32)
        others = jax.random.permutation(rest_key, (N_ADAPTER - 1) * CAP)[:REQUESTS_PER_ROW - CAP].astype(jnp.int32)
        owners_rest = (others // CAP + busiest + 1) % N_ADAPTER
        owners = jnp.concatenate([jnp.full((CAP,), busiest, jnp.int32), owners_rest])
        owners = jax.random.permutation(order_key, owners)
        slot_index = jax.random.randint(slot_key, (REQUESTS_PER_ROW,), 0, held_adapter_count).astype(jnp.int32)
        return inverse[owners * held_adapter_count + slot_index]
    requests = jax.vmap(one_run)(jax.random.split(run_key, N_ADAPTER))
    return (home_table, requests.astype(jnp.int32))


def draw_adapter_cache_row(key, part):
    home_table, requests = adapter_layout(key)
    return home_table


def draw_request_adapter_index(key, part):
    home_table, requests = adapter_layout(key)
    return requests


def draw_normed_hidden(key, part):
    key = jax.random.fold_in(key, 1)
    normal_key = jax.random.fold_in(key, 0)
    values = jnp.clip(jax.random.normal(normal_key, (TOKEN_TOTAL, MODEL_WIDTH), jnp.float32), -5.0, 5.0)
    return values.astype(jnp.bfloat16)


def steps_of(own_key, extent, shards, low, top_value):
    level = 1.0
    for axis_at, blocks in shards:
        heights = jax.random.uniform(jax.random.fold_in(jax.random.fold_in(own_key, 6), axis_at), (blocks,), jnp.float32, low / len(shards), top_value / len(shards))
        level = level * jnp.repeat(jnp.exp(heights), extent[axis_at] // blocks).reshape((-1,) + (1,) * (len(extent) - 1 - axis_at))
    return level


def profile(count, total, limit, lean):
    portions = [(1 << 20) // math.isqrt(standing ** lean) + 1 for standing in range(2, count + 1)]
    rest, holding = total - limit - (count - 1), [1] * (count - 1)
    while rest > 0:
        movable = [i for i in range(count - 1) if holding[i] < limit]
        mass, left = sum([portions[i] for i in movable]), rest
        for i in movable:
            addition = min(limit - holding[i], max(1, left * portions[i] // mass), rest)
            holding[i] = holding[i] + addition
            rest = rest - addition
    return np.array([limit] + holding)


def uneven_parts(stream_key, amount, total, most, skew):
    if amount == 2:
        one = jax.random.randint(stream_key, (), max(1, total - most), min(most, total - 1) + 1)
        return jnp.stack([one, total - one])
    sizes = jnp.asarray(profile(amount, total, most, skew), jnp.int32)
    couples = (amount - 1) // 2
    giver, receiver = sizes[1:1 + 2 * couples:2], sizes[2:2 + 2 * couples:2]
    margin = jnp.minimum(giver - 1, most - receiver)
    passed = jax.random.randint(jax.random.fold_in(stream_key, 1), (couples,), 0, 1 << 20) % (margin + 1)
    sizes = sizes.at[1:1 + 2 * couples:2].set(giver - passed).at[2:2 + 2 * couples:2].set(receiver + passed)
    return sizes[jax.random.permutation(jax.random.fold_in(stream_key, 2), amount)]


def noise(own_key, dims, width, reach, shards=(), kind=jnp.bfloat16):
    entries = width * jax.random.normal(own_key, dims, jnp.float32)
    if shards:
        entries = entries * steps_of(own_key, dims, shards, -0.22, 0.18)
    return jnp.clip(entries, -reach, reach).astype(kind)


def setup_inputs(seed: int = 0, part: int = 0) -> dict:
    key_of = jax.random.split(jax.random.key(seed), 13)
    part_splits = jax.random.split(jax.random.fold_in(key_of[12], part), 13)
    normed_hidden = draw_normed_hidden(jax.random.fold_in(jax.random.fold_in(key_of[12], part), 71), part)
    query_weight = noise(key_of[1], (MODEL_WIDTH, QUERY_HEADS * HEAD_WIDTH), MODEL_WIDTH ** -0.5, 0.09375, ((1, 4),))
    key_value_weight = noise(key_of[2], (2, MODEL_WIDTH, KEY_VALUE_HEADS * HEAD_WIDTH), MODEL_WIDTH ** -0.5, 0.09375, ((2, 4),))
    output_weight = noise(key_of[3], (QUERY_HEADS * HEAD_WIDTH, MODEL_WIDTH), (QUERY_HEADS * HEAD_WIDTH) ** -0.5, 0.09375, ((0, 4),))
    adapter_down_rows = noise(part_splits[4], (ADAPTER_COUNT, 3 * ADAPTER_RANK, MODEL_WIDTH), MODEL_WIDTH ** -0.5, 0.09375, ((0, 4),))
    adapter_query_up = noise(part_splits[5], (ADAPTER_COUNT, ADAPTER_RANK, QUERY_HEADS * HEAD_WIDTH), ADAPTER_RANK ** -0.5, 1.5, ((0, 4), (2, 4)))
    adapter_key_value_up = noise(part_splits[6], (ADAPTER_COUNT, 2, ADAPTER_RANK, KEY_VALUE_HEADS * HEAD_WIDTH), ADAPTER_RANK ** -0.5, 1.5, ((0, 4), (3, 4)))
    adapter_output_down = noise(part_splits[7], (ADAPTER_COUNT, ADAPTER_RANK, QUERY_HEADS * HEAD_WIDTH), (QUERY_HEADS * HEAD_WIDTH) ** -0.5, 0.09375, ((0, 4), (2, 4)))
    adapter_output_up = noise(part_splits[8], (ADAPTER_COUNT, ADAPTER_RANK, MODEL_WIDTH), ADAPTER_RANK ** -0.5, 1.5, ((0, 4), (2, 4)))
    adapter_cache_row = draw_adapter_cache_row(jax.random.fold_in(jax.random.fold_in(key_of[12], part), 71), part)
    request_adapter_index = draw_request_adapter_index(jax.random.fold_in(jax.random.fold_in(key_of[12], part), 71), part)
    request_token_length = jax.vmap(lambda own: uneven_parts(own, REQUESTS_PER_ROW, TOKENS_PER_ROW, TOKENS_PER_ROW // 2, 2))(jax.random.split(part_splits[11], N_ADAPTER)).reshape((N_ADAPTER, REQUESTS_PER_ROW)).astype(jnp.int32)
    return dict(normed_hidden=normed_hidden, query_weight=query_weight, key_value_weight=key_value_weight, output_weight=output_weight, adapter_down_rows=adapter_down_rows, adapter_query_up=adapter_query_up, adapter_key_value_up=adapter_key_value_up, adapter_output_down=adapter_output_down, adapter_output_up=adapter_output_up, adapter_cache_row=adapter_cache_row, request_adapter_index=request_adapter_index, request_token_length=request_token_length)


SCORE_SCALE = 0.5
THETA = 500000.0
NEG_FILL = -1.0e30


def apply_rotation(values, token_position):
    half_width = values.shape[-1] // 2
    exponent = jnp.arange(half_width).astype(jnp.float32) * (2.0 / values.shape[-1])
    frequency = THETA ** (-exponent)
    angles = token_position.astype(jnp.float32)[:, None] * frequency[None, :]
    cosine = jnp.cos(angles)[:, None, :]
    sine_part = jnp.sin(angles)[:, None, :]
    front_part = values[..., :half_width]
    back_part = values[..., half_width:]
    return jnp.concatenate([front_part * cosine - back_part * sine_part, back_part * cosine + front_part * sine_part], axis=-1)


def request_layout(lengths, token_count):
    ending = jnp.cumsum(lengths).astype(jnp.int32)
    starting = (ending - lengths).astype(jnp.int32)
    token_index = jnp.arange(token_count, dtype=jnp.int32)
    segment = jnp.sum((token_index[:, None] >= ending[None, :]).astype(jnp.int32), axis=1).astype(jnp.int32)
    member = segment[:, None] == jnp.arange(lengths.shape[0], dtype=jnp.int32)[None, :]
    token_position = (token_index - jnp.sum(jnp.where(member, starting[None, :], 0), axis=1)).astype(jnp.int32)
    return segment, token_position, member


def reference(normed_hidden, query_weight, key_value_weight, output_weight, adapter_down_rows, adapter_query_up, adapter_key_value_up, adapter_output_down, adapter_output_up, adapter_cache_row, request_adapter_index, request_token_length):
    query_group_width = QUERY_HEADS // KEY_VALUE_HEADS

    def one_run(inputs):
        x_run, run_adapters, run_lengths = inputs
        segment, token_position, member = request_layout(run_lengths, TOKENS_PER_ROW)
        holder_rows = adapter_cache_row[run_adapters]
        member_low = member.astype(jnp.bfloat16)

        def spread(low_part):
            return (member_low[:, :, None] * low_part[:, None, :]).reshape(TOKENS_PER_ROW, REQUESTS_PER_ROW * ADAPTER_RANK)

        request_down = adapter_down_rows[holder_rows].astype(jnp.float32)
        every_low = jnp.einsum("td,jrd->tjr", x_run.astype(jnp.float32), request_down)
        low_in = jnp.sum(jnp.where(member[:, :, None], every_low, 0.0), axis=1).astype(jnp.bfloat16)
        query_up_weight = adapter_query_up[holder_rows].reshape(REQUESTS_PER_ROW * ADAPTER_RANK, QUERY_HEADS * HEAD_WIDTH)
        key_value_up = adapter_key_value_up[holder_rows]
        key_up_weight = key_value_up[:, 0].reshape(REQUESTS_PER_ROW * ADAPTER_RANK, KEY_VALUE_HEADS * HEAD_WIDTH)
        value_up_weight = key_value_up[:, 1].reshape(REQUESTS_PER_ROW * ADAPTER_RANK, KEY_VALUE_HEADS * HEAD_WIDTH)
        query_lin = jnp.dot(x_run, query_weight, preferred_element_type=jnp.float32) + SCORE_SCALE * jnp.dot(spread(low_in[:, 0:ADAPTER_RANK]), query_up_weight, preferred_element_type=jnp.float32)
        key_linear = jnp.dot(x_run, key_value_weight[0], preferred_element_type=jnp.float32) + SCORE_SCALE * jnp.dot(spread(low_in[:, ADAPTER_RANK:2 * ADAPTER_RANK]), key_up_weight, preferred_element_type=jnp.float32)
        value_linear = jnp.dot(x_run, key_value_weight[1], preferred_element_type=jnp.float32) + SCORE_SCALE * jnp.dot(spread(low_in[:, 2 * ADAPTER_RANK:3 * ADAPTER_RANK]), value_up_weight, preferred_element_type=jnp.float32)
        query_head_rows = apply_rotation(query_lin.reshape(TOKENS_PER_ROW, QUERY_HEADS, HEAD_WIDTH), token_position).astype(jnp.bfloat16)
        key_head_rows = apply_rotation(key_linear.reshape(TOKENS_PER_ROW, KEY_VALUE_HEADS, HEAD_WIDTH), token_position).astype(jnp.bfloat16)
        value_head_rows = value_linear.astype(jnp.bfloat16).reshape(TOKENS_PER_ROW, KEY_VALUE_HEADS, HEAD_WIDTH)
        token_index = jnp.arange(TOKENS_PER_ROW, dtype=jnp.int32)
        allowed = (segment[:, None] == segment[None, :]) & (token_index[None, :] <= token_index[:, None])
        attention_scores = jnp.einsum("hoyr,lor->oyhl", query_head_rows.reshape(TOKENS_PER_ROW, KEY_VALUE_HEADS, query_group_width, HEAD_WIDTH).astype(jnp.float32), key_head_rows.astype(jnp.float32)) * (HEAD_WIDTH ** -0.5)
        attention_scores = jnp.where(allowed[None, None], attention_scores, NEG_FILL)
        maximum = jnp.max(attention_scores, axis=-1, keepdims=True)
        exponent_part = jnp.exp(attention_scores - maximum)
        weights = (exponent_part / jnp.sum(exponent_part, axis=-1, keepdims=True)).astype(jnp.bfloat16)
        attended = jnp.einsum("kgts,skd->tkgd", weights.astype(jnp.float32), value_head_rows.astype(jnp.float32)).reshape(TOKENS_PER_ROW, QUERY_HEADS * HEAD_WIDTH).astype(jnp.bfloat16)
        output_down = adapter_output_down[holder_rows].astype(jnp.float32)
        every_out = jnp.einsum("tc,jrc->tjr", attended.astype(jnp.float32), output_down)
        low_out = jnp.sum(jnp.where(member[:, :, None], every_out, 0.0), axis=1).astype(jnp.bfloat16)
        output_up = adapter_output_up[holder_rows].reshape(REQUESTS_PER_ROW * ADAPTER_RANK, MODEL_WIDTH)
        mixed_run = (jnp.dot(attended, output_weight, preferred_element_type=jnp.float32) + SCORE_SCALE * jnp.dot(spread(low_out), output_up, preferred_element_type=jnp.float32)).astype(jnp.bfloat16)
        cache_pass = jnp.stack([key_head_rows.reshape(TOKENS_PER_ROW, KEY_VALUE_HEADS * HEAD_WIDTH), value_head_rows.reshape(TOKENS_PER_ROW, KEY_VALUE_HEADS * HEAD_WIDTH)], axis=0)
        return mixed_run, cache_pass

    mixed, adapter_cache = lax.map(one_run, (normed_hidden.reshape(N_ADAPTER, TOKENS_PER_ROW, MODEL_WIDTH), request_adapter_index, request_token_length))
    return mixed.reshape(TOKEN_TOTAL, MODEL_WIDTH), jnp.transpose(adapter_cache, (1, 0, 2, 3)).reshape(2, TOKEN_TOTAL, KEY_VALUE_HEADS * HEAD_WIDTH)
```

```python
import jax
import jax.numpy as jnp
from jax import lax
from jax.sharding import PartitionSpec as P

HEAD_WIDTH = 128
CAP = 2
CHUNKS = 2


SCORE_SCALE = 0.5
THETA = 500000.0
NEG_FILL = -1e30


def rotation_tables(token_position):
    half_width = HEAD_WIDTH // 2
    exponent = jnp.arange(half_width).astype(jnp.float32) * (2.0 / HEAD_WIDTH)
    frequency = THETA ** (-exponent)
    angles = token_position.astype(jnp.float32)[:, None] * frequency[None, :]
    return jnp.cos(angles)[:, None, :], jnp.sin(angles)[:, None, :]


def apply_rotation(values, cosine, sine_part):
    half_width = values.shape[-1] // 2
    front_part = values[..., :half_width]
    back_part = values[..., half_width:]
    return jnp.concatenate(
        [front_part * cosine - back_part * sine_part, back_part * cosine + front_part * sine_part],
        axis=-1,
    )


def request_layout(lengths, token_count):
    ending = jnp.cumsum(lengths)
    starting = ending - lengths
    token_index = jnp.arange(token_count, dtype=jnp.int32)
    segment = jnp.sum((token_index[:, None] >= ending[None, :]).astype(jnp.int32), axis=1)
    member = segment[:, None] == jnp.arange(lengths.shape[0], dtype=jnp.int32)[None, :]
    token_position = token_index - jnp.sum(jnp.where(member, starting[None, :], 0), axis=1)
    return (segment, token_position, member)


def after(value, *others):
    return lax.optimization_barrier((value,) + others)[0]


def line_gather(own, me, count, previous):
    width = own.shape[1]
    right = left = own if previous is None else after(own, *previous)
    from_left, from_right, marks = [None], [None], []
    for step in range(1, count):
        right = lax.ppermute(right, "tensor", [(i, i + 1) for i in range(step - 1, count - 1)])
        left = lax.ppermute(left, "tensor", [(i, i - 1) for i in range(1, count - step + 1)])
        from_left.append(right)
        from_right.append(left)
        if step == max(1, count - 2):
            marks = (right, left)
    whole = jnp.zeros((own.shape[0], width * count), own.dtype)
    whole = lax.dynamic_update_slice(whole, own, (0, me * width))
    for k in range(1, count):
        block = jnp.where(me + k < count, from_right[k], from_left[count - k])
        whole = lax.dynamic_update_slice(whole, block, (0, ((me + k) % count) * width))
    return whole, marks


def line_reduce(partial, me, count):
    width = partial.shape[1] // count

    def block(index):
        return lax.dynamic_slice(partial, (0, index * width), (partial.shape[0], width))

    right = left = None
    for step in range(1, count):
        to_right = block((me + count - step) % count)
        to_left = block((me + step) % count)
        if right is not None:
            to_right = to_right + right.astype(jnp.float32)
            to_left = to_left + left.astype(jnp.float32)
        right = lax.ppermute(
            to_right.astype(jnp.bfloat16), "tensor", [(i, i + 1) for i in range(min(step, count - 1))]
        )
        left = lax.ppermute(
            to_left.astype(jnp.bfloat16), "tensor", [(i, i - 1) for i in range(count - step, count)]
        )
    return block(me) + right.astype(jnp.float32) + left.astype(jnp.float32)


def small_sum(own, count):
    total = own
    for k in range(1, count):
        total = total + lax.ppermute(own, "tensor", [(i, (i + k) % count) for i in range(count)])
    return total


def local(
    normed_hidden,
    query_weight,
    key_value_weight,
    output_weight,
    adapter_down_rows,
    adapter_query_up,
    adapter_key_value_up,
    adapter_output_down,
    adapter_output_up,
    adapter_cache_row,
    request_adapter_index,
    request_token_length,
):
    token_count = normed_hidden.shape[0]
    slice_width = normed_hidden.shape[1]
    rank = adapter_query_up.shape[1]
    held_adapter_count = adapter_down_rows.shape[0]
    owner_count = lax.axis_size("adapter")
    count = lax.axis_size("tensor")
    me = lax.axis_index("tensor")
    query_cols = query_weight.shape[1]
    keyval_cols = key_value_weight.shape[2]
    query_local = query_cols // HEAD_WIDTH
    keyval_local = keyval_cols // HEAD_WIDTH
    query_group_width = query_local // keyval_local
    size = token_count // CHUNKS

    gathered, marks = [], None
    for c in range(CHUNKS):
        whole, marks = line_gather(normed_hidden[c * size : (c + 1) * size], me, count, marks)
        gathered.append(whole)

    request_ids = request_adapter_index[0]
    lengths = request_token_length[0]
    request_count = request_ids.shape[0]
    catalog = jnp.arange(adapter_cache_row.shape[0], dtype=jnp.int32)
    holder_rows = jnp.sum(
        jnp.where(request_ids[:, None] == catalog[None, :], adapter_cache_row[None, :], 0), axis=1
    )
    owner_index = holder_rows // held_adapter_count
    local_slot = holder_rows % held_adapter_count
    request_order = jnp.arange(request_count, dtype=jnp.int32)
    earlier = (owner_index[:, None] == owner_index[None, :]) & (
        request_order[None, :] < request_order[:, None]
    )
    rank_within = jnp.sum(earlier.astype(jnp.int32), axis=1)
    placed = owner_index * CAP + rank_within
    targets = jnp.arange(owner_count * CAP, dtype=jnp.int32)
    want_table = jnp.sum(
        jnp.where(placed[:, None] == targets[None, :], local_slot[:, None], 0), axis=0
    )
    want_table = want_table.reshape(owner_count, CAP)
    picked = lax.all_to_all(want_table, "adapter", split_axis=0, concat_axis=0, tiled=True)

    def fetch(rows):
        received = lax.all_to_all(rows, "adapter", split_axis=0, concat_axis=0, tiled=True)
        received = received.reshape((owner_count * CAP,) + rows.shape[2:])
        return jnp.take(received, placed, axis=0)

    req_down = fetch(jnp.take(adapter_down_rows, picked, axis=0))
    small = fetch(
        jnp.concatenate(
            [
                jnp.take(adapter_query_up, picked, axis=0),
                jnp.take(adapter_key_value_up[:, 0], picked, axis=0),
                jnp.take(adapter_key_value_up[:, 1], picked, axis=0),
                jnp.take(adapter_output_down, picked, axis=0),
                jnp.take(adapter_output_up, picked, axis=0),
            ],
            axis=-1,
        )
    )
    flat_rank = request_count * rank
    cuts, at = [], 0
    for width in (query_cols, keyval_cols, keyval_cols, query_cols, slice_width):
        cuts.append(small[:, :, at : at + width].reshape(flat_rank, width))
        at += width
    query_up, key_up, value_up, out_down, out_up = cuts

    segment, token_position, member = request_layout(lengths, token_count)
    cosine, sine_part = rotation_tables(token_position)
    token_index = jnp.arange(token_count, dtype=jnp.int32)

    mixed, keys, values = [], [], []
    for c in range(CHUNKS):
        part = slice(c * size, (c + 1) * size)
        member_c = member[part]
        member_low = member_c.astype(jnp.bfloat16)

        def spread(low_part):
            return (member_low[:, :, None] * low_part[:, None, :]).reshape(size, flat_rank)

        x = gathered[c]
        low_next = jnp.einsum("td,jrd->tjr", x, req_down, preferred_element_type=jnp.float32)
        low_in = jnp.sum(jnp.where(member_c[:, :, None], low_next, 0.0), axis=1).astype(jnp.bfloat16)

        def projected(weight, low_part, up):
            return jnp.dot(x, weight, preferred_element_type=jnp.float32) + SCORE_SCALE * jnp.dot(
                spread(low_part), up, preferred_element_type=jnp.float32
            )

        query_lin = projected(query_weight, low_in[:, 0:rank], query_up)
        key_linear = projected(key_value_weight[0], low_in[:, rank : 2 * rank], key_up)
        value_linear = projected(key_value_weight[1], low_in[:, 2 * rank : 3 * rank], value_up)
        query_rows = apply_rotation(
            query_lin.reshape(size, query_local, HEAD_WIDTH), cosine[part], sine_part[part]
        ).astype(jnp.bfloat16)
        key_rows = apply_rotation(
            key_linear.reshape(size, keyval_local, HEAD_WIDTH), cosine[part], sine_part[part]
        ).astype(jnp.bfloat16)
        keys.append(key_rows)
        values.append(value_linear.astype(jnp.bfloat16).reshape(size, keyval_local, HEAD_WIDTH))
        reach = (c + 1) * size
        all_keys = jnp.concatenate(keys, axis=0)
        all_values = jnp.concatenate(values, axis=0)
        allowed = (segment[part][:, None] == segment[None, :reach]) & (
            token_index[None, :reach] <= token_index[part][:, None]
        )
        scores = (
            jnp.einsum(
                "hoyr,lor->oyhl",
                query_rows.reshape(size, keyval_local, query_group_width, HEAD_WIDTH),
                all_keys,
                preferred_element_type=jnp.float32,
            )
            * HEAD_WIDTH ** (-0.5)
        )
        scores = jnp.where(allowed[None, None], scores, NEG_FILL)
        maximum = jnp.max(scores, axis=-1, keepdims=True)
        exponent_part = jnp.exp(scores - maximum)
        weights = (exponent_part / jnp.sum(exponent_part, axis=-1, keepdims=True)).astype(jnp.bfloat16)
        attended = (
            jnp.einsum("kgts,skd->tkgd", weights, all_values, preferred_element_type=jnp.float32)
            .reshape(size, query_cols)
            .astype(jnp.bfloat16)
        )
        partial = jnp.dot(attended, output_weight, preferred_element_type=jnp.float32)
        base_output = line_reduce(partial, me, count)
        partial_low = jnp.dot(
            attended, out_down.T, preferred_element_type=jnp.float32
        ).reshape(size, request_count, rank)
        picked_out = jnp.sum(jnp.where(member_c[:, :, None], partial_low, 0.0), axis=1)
        low_out = small_sum(picked_out, count).astype(jnp.bfloat16)
        adapter_term = jnp.dot(spread(low_out), out_up, preferred_element_type=jnp.float32)
        mixed.append((base_output + SCORE_SCALE * adapter_term).astype(jnp.bfloat16))

    kv_cache = jnp.stack(
        [
            jnp.concatenate(keys, axis=0).reshape(token_count, keyval_cols),
            jnp.concatenate(values, axis=0).reshape(token_count, keyval_cols),
        ],
        axis=0,
    )
    return (jnp.concatenate(mixed, axis=0), kv_cache)


def solution(mesh):
    in_specs = (
        P(("groups", "adapter"), "tensor"),
        P(None, "tensor"),
        P(None, None, "tensor"),
        P("tensor", None),
        P(("groups", "adapter"), None, None),
        P(("groups", "adapter"), None, "tensor"),
        P(("groups", "adapter"), None, None, "tensor"),
        P(("groups", "adapter"), None, "tensor"),
        P(("groups", "adapter"), None, "tensor"),
        P("groups"),
        P(("groups", "adapter"), None),
        P(("groups", "adapter"), None),
    )
    out_specs = (P(("groups", "adapter"), "tensor"), P(None, ("groups", "adapter"), "tensor"))
    return jax.shard_map(local, mesh=mesh, in_specs=in_specs, out_specs=out_specs, check_vma=False)
```

```python
import functools
import jax
import jax.numpy as jnp
from jax import lax
from jax.experimental import pallas as pl
from jax.experimental.pallas import tpu as pltpu
from jax.sharding import PartitionSpec as P

HEAD_WIDTH = 128
CAP = 2
CHUNKS = 4
LANES = 128


SCORE_SCALE = 0.5
THETA = 500000.0
NEG_FILL = -1e30
MESH = pl.DeviceIdType.MESH


def rotation_tables(token_position):
    half_width = HEAD_WIDTH // 2
    exponent = jnp.arange(half_width).astype(jnp.float32) * (2.0 / HEAD_WIDTH)
    frequency = THETA ** (-exponent)
    angles = token_position.astype(jnp.float32)[:, None] * frequency[None, :]
    cosine, sine_part = jnp.cos(angles), jnp.sin(angles)
    return (
        jnp.concatenate([cosine, cosine], axis=1),
        jnp.concatenate([-sine_part, sine_part], axis=1),
    )


def layer_kernel(
    count, owners, rank, mine_x, wq_in, wkv_in, wo_in, down_in, small_in, cos_ref, sin_ref,
    mask_ref, seg_ref, seg_row, mixed_ref, kv_ref,
    xg, wq, wkv, wo, down, small, query, att, acc, rs_out, rs_in, low_out, low_in,
    ag_send, ag_recv, rs_send, rs_recv, lo_send, lo_recv, ad_send, ad_recv, here,
):
    me = lax.axis_index("tensor")
    home = lax.axis_index("adapter")
    tokens, width = mine_x.shape
    size = tokens // CHUNKS
    query_cols = wq.shape[1]
    keyval_cols = wkv.shape[2]
    slots = small.shape[0] * small.shape[1]
    group = query_cols // keyval_cols
    dot = functools.partial(jnp.dot, preferred_element_type=jnp.float32)

    def dot_t(a, b):
        return lax.dot_general(a, b, (((1,), (1,)), ((), ())), preferred_element_type=jnp.float32)

    barrier = pltpu.get_barrier_semaphore()
    for k in range(1, count):
        pl.semaphore_signal(
            barrier, inc=1, device_id={"tensor": lax.rem(me + k, count)}, device_id_type=MESH
        )
    for k in range(1, owners):
        pl.semaphore_signal(
            barrier, inc=1, device_id={"adapter": lax.rem(home + k, owners)}, device_id_type=MESH
        )
    pl.semaphore_wait(barrier, count - 1 + owners - 1)

    def rows(c):
        return pl.ds(c * size, size)

    def columns(j):
        return pl.ds(pl.multiple_of(j * width, width), width)

    def gather_copy(way, hop, c, receiving):
        source = me - hop if way == 0 else me + hop
        source = source if receiving else (source + 1 if way == 0 else source - 1)
        place = xg.at[rows(c), columns(source)]
        return pltpu.make_async_remote_copy(
            src_ref=mine_x.at[rows(c), :] if hop == 1 else place,
            dst_ref=place,
            send_sem=ag_send.at[way, hop - 1, c],
            recv_sem=ag_recv.at[way, hop - 1, c],
            device_id={"tensor": me + 1 if way == 0 else me - 1},
            device_id_type=MESH,
        )

    def sends_gather(way, hop):
        if way == 0:
            return jnp.logical_and(me >= hop - 1, me < count - 1)
        return jnp.logical_and(me <= count - hop, me > 0)

    def takes_gather(way, hop):
        return me >= hop if way == 0 else me <= count - 1 - hop

    def send_gather(c, hop):
        for way in range(2):
            @pl.when(sends_gather(way, hop))
            def _():
                gather_copy(way, hop, c, False).start()

    def take_gather(c, hop):
        for way in range(2):
            @pl.when(takes_gather(way, hop))
            def _():
                gather_copy(way, hop, c, True).wait_recv()
        if hop < count - 1:
            send_gather(c, hop + 1)

    def adapter_copy(k, kind):
        source, place = (down_in, down) if kind == 0 else (small_in, small)
        there = lax.rem(home + k, owners)
        if kind == 0:
            src, dst = source.at[there], place.at[:, home]
        else:
            src, dst = source.at[there], place.at[home]
        return pltpu.make_async_remote_copy(
            src_ref=src,
            dst_ref=dst,
            send_sem=ad_send.at[k - 1, kind],
            recv_sem=ad_recv.at[k - 1, kind],
            device_id={"adapter": there},
            device_id_type=MESH,
        )

    locals_ = [
        pltpu.make_async_copy(mine_x, xg.at[:, columns(me)], here.at[0]),
        pltpu.make_async_copy(down_in.at[home], down.at[:, home], here.at[1]),
        pltpu.make_async_copy(small_in.at[home], small.at[home], here.at[2]),
        pltpu.make_async_copy(wq_in, wq, here.at[3]),
        pltpu.make_async_copy(wkv_in, wkv, here.at[4]),
        pltpu.make_async_copy(wo_in, wo, here.at[5]),
    ]
    send_gather(0, 1)
    for k in range(1, owners):
        adapter_copy(k, 0).start()
        adapter_copy(k, 1).start()
    for copy in locals_:
        copy.start()
    send_gather(1, 1)
    for hop in range(1, count):
        take_gather(0, hop)
    for copy in locals_:
        copy.wait()
    for k in range(1, owners):
        adapter_copy(k, 0).wait_recv()
        adapter_copy(k, 1).wait_recv()

    ups = small.shape[2]
    at_query, at_key, at_value = 0, query_cols, query_cols + keyval_cols
    at_down = at_value + keyval_cols
    at_up = at_down + query_cols

    def small_rows(start, extent):
        return small[:, :, start : start + extent].reshape(slots, extent)

    def rotate(values, c):
        half = HEAD_WIDTH // 2
        swapped = jnp.concatenate([values[:, half:], values[:, :half]], axis=1)
        return values * cos_ref[rows(c), :] + swapped * sin_ref[rows(c), :]

    def low_part(c):
        low = dot_t(xg[rows(c), :], down[...].reshape(3 * slots, down.shape[3]))
        mask = mask_ref[rows(c), :]
        return [
            jnp.where(mask > 0, low[:, i * slots : (i + 1) * slots], 0.0).astype(jnp.bfloat16)
            for i in range(3)
        ]

    def query_part(c, low):
        for h in range(0, query_cols, 2 * HEAD_WIDTH):
            lin = dot(xg[rows(c), :], wq[:, h : h + 2 * HEAD_WIDTH]) + SCORE_SCALE * dot(
                low, small_rows(at_query + h, 2 * HEAD_WIDTH)
            )
            for i in range(2):
                piece = rotate(lin[:, i * HEAD_WIDTH : (i + 1) * HEAD_WIDTH], c)
                query[:, h + i * HEAD_WIDTH : h + (i + 1) * HEAD_WIDTH] = piece.astype(jnp.bfloat16)

    def keyval_part(c, low_key, low_value):
        key = dot(xg[rows(c), :], wkv[0]) + SCORE_SCALE * dot(
            low_key, small_rows(at_key, keyval_cols)
        )
        for h in range(0, keyval_cols, HEAD_WIDTH):
            kv_ref[0, rows(c), h : h + HEAD_WIDTH] = rotate(key[:, h : h + HEAD_WIDTH], c).astype(
                jnp.bfloat16
            )
        value = dot(xg[rows(c), :], wkv[1]) + SCORE_SCALE * dot(
            low_value, small_rows(at_value, keyval_cols)
        )
        kv_ref[1, rows(c), :] = value.astype(jnp.bfloat16)

    def attention_part(c, g):
        reach = (c + 1) * size
        t_index = c * size + lax.broadcasted_iota(jnp.int32, (size, reach), 0)
        s_index = lax.broadcasted_iota(jnp.int32, (size, reach), 1)
        allowed = jnp.logical_and(
            seg_ref[rows(c), :] == seg_row[:, :reach], s_index <= t_index
        )
        head = slice(g * HEAD_WIDTH, (g + 1) * HEAD_WIDTH)
        key = kv_ref[0, :reach, head]
        value = kv_ref[1, :reach, head]
        for i in range(group):
            spot = slice((g * group + i) * HEAD_WIDTH, (g * group + i + 1) * HEAD_WIDTH)
            scores = dot_t(query[:, spot], key) * HEAD_WIDTH ** (-0.5)
            scores = jnp.where(allowed, scores, NEG_FILL)
            grown = jnp.exp(scores - jnp.max(scores, axis=-1, keepdims=True))
            weights = (grown / jnp.sum(grown, axis=-1, keepdims=True)).astype(jnp.bfloat16)
            att[rows(c), spot] = dot(weights, value).astype(jnp.bfloat16)

    def reduce_copy(way, step, c):
        return pltpu.make_async_remote_copy(
            src_ref=rs_out.at[way, step - 1, c],
            dst_ref=rs_in.at[way, step - 1, c],
            send_sem=rs_send.at[way, step - 1, c],
            recv_sem=rs_recv.at[way, step - 1, c],
            device_id={"tensor": me + 1 if way == 0 else me - 1},
            device_id_type=MESH,
        )

    def sends_reduce(way, step):
        return me <= step - 1 if way == 0 else me >= count - step

    def has_before(way):
        return me >= 1 if way == 0 else me <= count - 2

    def reduce_step(c, step):
        for way in range(2):
            @pl.when(sends_reduce(way, step))
            def _():
                block = me + count - step if way == 0 else me - count + step
                acc[...] = dot(att[rows(c), :], wo[:, columns(block)])
                if step > 1:
                    @pl.when(has_before(way))
                    def _():
                        reduce_copy(way, step - 1, c).wait_recv()
                        acc[...] += rs_in[way, step - 2, c].astype(jnp.float32)
                rs_out[way, step - 1, c] = acc[...].astype(jnp.bfloat16)
                reduce_copy(way, step, c).start()

    def low_copy(k, c, receiving):
        place = lax.rem(me + count - k, count) if receiving else me
        return pltpu.make_async_remote_copy(
            src_ref=low_out.at[c],
            dst_ref=low_in.at[c, place],
            send_sem=lo_send.at[k - 1, c],
            recv_sem=lo_recv.at[k - 1, c],
            device_id={"tensor": lax.rem(me + k, count)},
            device_id_type=MESH,
        )

    per = LANES // rank
    packed_rows = size // per

    def low_send(c):
        part = dot_t(att[rows(c), :], small_rows(at_down, query_cols))
        part = jnp.where(mask_ref[rows(c), :] > 0, part, 0.0)
        total = part[:, 0:rank]
        for s in range(1, slots // rank):
            total = total + part[:, s * rank : (s + 1) * rank]
        packed = jnp.concatenate(
            [total[i * packed_rows : (i + 1) * packed_rows] for i in range(per)], axis=1
        )
        low_out[c] = packed
        low_in[c, me] = packed
        for k in range(1, count):
            low_copy(k, c, False).start()

    def finish(c):
        acc[...] = dot(att[rows(c), :], wo[:, columns(me)])
        for k in range(1, count):
            low_copy(k, c, True).wait_recv()
        packed = low_in[c, 0]
        for j in range(1, count):
            packed = packed + low_in[c, j]
        low = jnp.concatenate([packed[:, i * rank : (i + 1) * rank] for i in range(per)], axis=0)
        low = jnp.concatenate([low] * (slots // rank), axis=1)
        low = jnp.where(mask_ref[rows(c), :] > 0, low, 0.0).astype(jnp.bfloat16)
        acc[...] += SCORE_SCALE * dot(low, small_rows(at_up, width))
        for way in range(2):
            @pl.when(has_before(way))
            def _():
                reduce_copy(way, count - 1, c).wait_recv()
                acc[...] += rs_in[way, count - 2, c].astype(jnp.float32)
        mixed_ref[rows(c), :] = acc[...].astype(jnp.bfloat16)

    for c in range(CHUNKS):
        if c + 2 < CHUNKS:
            send_gather(c + 2, 1)
        lows = low_part(c)
        work = [
            lambda: keyval_part(c, lows[1], lows[2]),
            lambda: query_part(c, lows[0]),
        ] + [functools.partial(attention_part, c, g) for g in range(keyval_cols // HEAD_WIDTH)]
        for i in range(max(len(work), count)):
            hop = i + 1
            if hop < count:
                if c >= 1:
                    reduce_step(c - 1, hop)
                if c + 1 < CHUNKS:
                    take_gather(c + 1, hop)
            if i < len(work):
                work[i]()
        low_send(c)
        if c >= 1:
            finish(c - 1)
    for step in range(1, count):
        reduce_step(CHUNKS - 1, step)
    finish(CHUNKS - 1)

    for c in range(CHUNKS):
        for hop in range(1, count):
            for way in range(2):
                @pl.when(sends_gather(way, hop))
                def _():
                    gather_copy(way, hop, c, False).wait_send()

                @pl.when(sends_reduce(way, hop))
                def _():
                    reduce_copy(way, hop, c).wait_send()
            low_copy(hop, c, False).wait_send()
    for k in range(1, owners):
        adapter_copy(k, 0).wait_send()
        adapter_copy(k, 1).wait_send()


def local(
    normed_hidden,
    query_weight,
    key_value_weight,
    output_weight,
    adapter_down_rows,
    adapter_query_up,
    adapter_key_value_up,
    adapter_output_down,
    adapter_output_up,
    adapter_cache_row,
    request_adapter_index,
    request_token_length,
):
    token_count = normed_hidden.shape[0]
    slice_width = normed_hidden.shape[1]
    rank = adapter_query_up.shape[1]
    model_width = adapter_down_rows.shape[2]
    held_adapter_count = adapter_down_rows.shape[0]
    owners = lax.axis_size("adapter")
    count = lax.axis_size("tensor")
    query_cols = query_weight.shape[1]
    keyval_cols = key_value_weight.shape[2]
    size = token_count // CHUNKS

    request_ids = request_adapter_index[0]
    lengths = request_token_length[0]
    request_count = request_ids.shape[0]
    catalog = jnp.arange(adapter_cache_row.shape[0], dtype=jnp.int32)
    holder_rows = jnp.sum(
        jnp.where(request_ids[:, None] == catalog[None, :], adapter_cache_row[None, :], 0), axis=1
    )
    owner_index = holder_rows // held_adapter_count
    local_slot = holder_rows % held_adapter_count
    request_order = jnp.arange(request_count, dtype=jnp.int32)
    earlier = (owner_index[:, None] == owner_index[None, :]) & (
        request_order[None, :] < request_order[:, None]
    )
    rank_within = jnp.sum(earlier.astype(jnp.int32), axis=1)
    placed = owner_index * CAP + rank_within
    targets = jnp.arange(owners * CAP, dtype=jnp.int32)
    want_table = jnp.sum(
        jnp.where(placed[:, None] == targets[None, :], local_slot[:, None], 0), axis=0
    )
    picked = lax.all_to_all(
        want_table.reshape(owners, CAP), "adapter", split_axis=0, concat_axis=0, tiled=True
    )
    down = jnp.take(adapter_down_rows, picked, axis=0)
    down = down.reshape(owners, CAP, 3, rank, model_width).transpose(0, 2, 1, 3, 4)
    down = down.reshape(owners, 3, CAP * rank, model_width)
    small = jnp.concatenate(
        [
            jnp.take(adapter_query_up, picked, axis=0),
            jnp.take(adapter_key_value_up[:, 0], picked, axis=0),
            jnp.take(adapter_key_value_up[:, 1], picked, axis=0),
            jnp.take(adapter_output_down, picked, axis=0),
            jnp.take(adapter_output_up, picked, axis=0),
        ],
        axis=-1,
    )
    small_width = small.shape[-1]
    small = small.reshape(owners, CAP * rank, small_width)

    ending = jnp.cumsum(lengths)
    starting = ending - lengths
    token_index = jnp.arange(token_count, dtype=jnp.int32)
    segment = jnp.sum((token_index[:, None] >= ending[None, :]).astype(jnp.int32), axis=1)
    member = segment[:, None] == request_order[None, :]
    token_position = token_index - jnp.sum(jnp.where(member, starting[None, :], 0), axis=1)
    cosine, sine_part = rotation_tables(token_position)
    slot_of = jnp.sum(jnp.where(member, placed[None, :], 0), axis=1)
    slots = owners * CAP * rank
    mask = (slot_of[:, None] == (jnp.arange(slots, dtype=jnp.int32) // rank)[None, :]).astype(
        jnp.float32
    )

    any_spec = pl.BlockSpec(memory_space=pl.ANY)
    vmem = pl.BlockSpec(memory_space=pltpu.VMEM)
    packed = (size * rank // LANES, LANES)
    dma = pltpu.SemaphoreType.DMA
    mixed, kv_cache = pl.pallas_call(
        functools.partial(layer_kernel, count, owners, rank),
        out_shape=(
            jax.ShapeDtypeStruct((token_count, slice_width), jnp.bfloat16),
            jax.ShapeDtypeStruct((2, token_count, keyval_cols), jnp.bfloat16),
        ),
        in_specs=[any_spec] * 6 + [vmem] * 5,
        out_specs=(vmem, vmem),
        scratch_shapes=[
            pltpu.VMEM((token_count, model_width), jnp.bfloat16),
            pltpu.VMEM(query_weight.shape, jnp.bfloat16),
            pltpu.VMEM(key_value_weight.shape, jnp.bfloat16),
            pltpu.VMEM(output_weight.shape, jnp.bfloat16),
            pltpu.VMEM((3, owners, CAP * rank, model_width), jnp.bfloat16),
            pltpu.VMEM((owners, CAP * rank, small_width), jnp.bfloat16),
            pltpu.VMEM((size, query_cols), jnp.bfloat16),
            pltpu.VMEM((token_count, query_cols), jnp.bfloat16),
            pltpu.VMEM((size, slice_width), jnp.float32),
            pltpu.VMEM((2, count - 1, CHUNKS, size, slice_width), jnp.bfloat16),
            pltpu.VMEM((2, count - 1, CHUNKS, size, slice_width), jnp.bfloat16),
            pltpu.VMEM((CHUNKS,) + packed, jnp.float32),
            pltpu.VMEM((CHUNKS, count) + packed, jnp.float32),
            dma((2, count - 1, CHUNKS)),
            dma((2, count - 1, CHUNKS)),
            dma((2, count - 1, CHUNKS)),
            dma((2, count - 1, CHUNKS)),
            dma((count - 1, CHUNKS)),
            dma((count - 1, CHUNKS)),
            dma((owners - 1, 2)),
            dma((owners - 1, 2)),
            dma((6,)),
        ],
        compiler_params=pltpu.CompilerParams(
            collective_id=0, has_side_effects=True, vmem_limit_bytes=60 * 1024 * 1024
        ),
    )(
        normed_hidden, query_weight, key_value_weight, output_weight, down, small,
        cosine, sine_part, mask, segment[:, None], segment[None, :],
    )
    return (mixed, kv_cache)


def solution(mesh):
    in_specs = (
        P(("groups", "adapter"), "tensor"),
        P(None, "tensor"),
        P(None, None, "tensor"),
        P("tensor", None),
        P(("groups", "adapter"), None, None),
        P(("groups", "adapter"), None, "tensor"),
        P(("groups", "adapter"), None, None, "tensor"),
        P(("groups", "adapter"), None, "tensor"),
        P(("groups", "adapter"), None, "tensor"),
        P("groups"),
        P(("groups", "adapter"), None),
        P(("groups", "adapter"), None),
    )
    out_specs = (P(("groups", "adapter"), "tensor"), P(None, ("groups", "adapter"), "tensor"))
    return jax.shard_map(local, mesh=mesh, in_specs=in_specs, out_specs=out_specs, check_vma=False)
```

```python
import functools
import jax
import jax.numpy as jnp
from jax import lax
from jax.experimental import pallas as pl
from jax.experimental.pallas import tpu as pltpu
from jax.sharding import PartitionSpec as P

HEAD_WIDTH = 128
CAP = 2
CHUNKS = 4
LANES = 128


SCORE_SCALE = 0.5
THETA = 500000.0
NEG_FILL = -1e30
MESH = pl.DeviceIdType.MESH


def rotation_tables(token_position):
    half_width = HEAD_WIDTH // 2
    exponent = jnp.arange(half_width).astype(jnp.float32) * (2.0 / HEAD_WIDTH)
    frequency = THETA ** (-exponent)
    angles = token_position.astype(jnp.float32)[:, None] * frequency[None, :]
    cosine, sine_part = jnp.cos(angles), jnp.sin(angles)
    return (
        jnp.concatenate([cosine, cosine], axis=1),
        jnp.concatenate([-sine_part, sine_part], axis=1),
    )


def layer_kernel(
    count, owners, rank, mine_x, wq_in, wkv_in, wo_in, down_in, small_in, cos_ref, sin_ref,
    mask_ref, seg_ref, seg_row, mixed_ref, kv_ref,
    xg, wq, wkv, wo, down, small, query, base, att, acc, rs_out, rs_in, low_out, low_in, first_out, first_in,
    ag_send, ag_recv, rs_send, rs_recv, lo_send, lo_recv, fi_send, fi_recv, ad_send, ad_recv, here,
):
    me = lax.axis_index("tensor")
    home = lax.axis_index("adapter")
    tokens, width = mine_x.shape
    size = tokens // CHUNKS
    query_cols = wq.shape[1]
    keyval_cols = wkv.shape[2]
    slots = small.shape[0] * small.shape[1]
    group = query_cols // keyval_cols
    dot = functools.partial(jnp.dot, preferred_element_type=jnp.float32)

    def dot_t(a, b):
        return lax.dot_general(a, b, (((1,), (1,)), ((), ())), preferred_element_type=jnp.float32)

    barrier = pltpu.get_barrier_semaphore()
    for k in range(1, count):
        pl.semaphore_signal(
            barrier, inc=1, device_id={"tensor": lax.rem(me + k, count)}, device_id_type=MESH
        )
    for k in range(1, owners):
        pl.semaphore_signal(
            barrier, inc=1, device_id={"adapter": lax.rem(home + k, owners)}, device_id_type=MESH
        )
    pl.semaphore_wait(barrier, count - 1 + owners - 1)

    def rows(c):
        return pl.ds(c * size, size)

    def columns(j):
        return pl.ds(pl.multiple_of(j * width, width), width)

    def gather_copy(way, hop, c, receiving):
        source = me - hop if way == 0 else me + hop
        source = source if receiving else (source + 1 if way == 0 else source - 1)
        place = xg.at[rows(c), columns(source)]
        return pltpu.make_async_remote_copy(
            src_ref=mine_x.at[rows(c), :] if hop == 1 else place,
            dst_ref=place,
            send_sem=ag_send.at[way, hop - 1, c],
            recv_sem=ag_recv.at[way, hop - 1, c],
            device_id={"tensor": me + 1 if way == 0 else me - 1},
            device_id_type=MESH,
        )

    def sends_gather(way, hop):
        if way == 0:
            return jnp.logical_and(me >= hop - 1, me < count - 1)
        return jnp.logical_and(me <= count - hop, me > 0)

    def takes_gather(way, hop):
        return me >= hop if way == 0 else me <= count - 1 - hop

    def send_gather(c, hop):
        for way in range(2):
            @pl.when(sends_gather(way, hop))
            def _():
                gather_copy(way, hop, c, False).start()

    def take_gather(c, hop):
        for way in range(2):
            @pl.when(takes_gather(way, hop))
            def _():
                gather_copy(way, hop, c, True).wait_recv()
        if hop < count - 1:
            send_gather(c, hop + 1)

    def adapter_copy(k, kind):
        source, place = (down_in, down) if kind == 0 else (small_in, small)
        there = lax.rem(home + k, owners)
        if kind == 0:
            src, dst = source.at[there], place.at[:, home]
        else:
            src, dst = source.at[there], place.at[home]
        return pltpu.make_async_remote_copy(
            src_ref=src,
            dst_ref=dst,
            send_sem=ad_send.at[k - 1, kind],
            recv_sem=ad_recv.at[k - 1, kind],
            device_id={"adapter": there},
            device_id_type=MESH,
        )

    locals_ = [
        pltpu.make_async_copy(mine_x, xg.at[:, columns(me)], here.at[0]),
        pltpu.make_async_copy(down_in.at[home], down.at[:, home], here.at[1]),
        pltpu.make_async_copy(small_in.at[home], small.at[home], here.at[2]),
        pltpu.make_async_copy(wq_in, wq, here.at[3]),
        pltpu.make_async_copy(wkv_in, wkv, here.at[4]),
        pltpu.make_async_copy(wo_in, wo, here.at[5]),
    ]
    send_gather(0, 1)
    for k in range(1, owners):
        adapter_copy(k, 0).start()
        adapter_copy(k, 1).start()
    for copy in locals_:
        copy.start()
    send_gather(1, 1)
    at_query, at_key, at_value = 0, query_cols, query_cols + keyval_cols
    at_down = at_value + keyval_cols
    at_up = at_down + query_cols

    def small_rows(start, extent):
        return small[:, :, start : start + extent].reshape(slots, extent)

    def rotate(values, c):
        half = HEAD_WIDTH // 2
        swapped = jnp.concatenate([values[:, half:], values[:, :half]], axis=1)
        return values * cos_ref[rows(c), :] + swapped * sin_ref[rows(c), :]

    per = LANES // rank
    packed_rows = size // per

    def pack(part):
        total = part[:, 0:rank]
        for s in range(1, slots // rank):
            total = total + part[:, s * rank : (s + 1) * rank]
        return jnp.concatenate(
            [total[i * packed_rows : (i + 1) * packed_rows] for i in range(per)], axis=1
        )

    def unpack(packed, c):
        low = jnp.concatenate([packed[:, i * rank : (i + 1) * rank] for i in range(per)], axis=0)
        low = jnp.concatenate([low] * (slots // rank), axis=1)
        return jnp.where(mask_ref[rows(c), :] > 0, low, 0.0).astype(jnp.bfloat16)

    def first_copy(k, receiving):
        place = lax.rem(me + count - k, count) if receiving else me
        return pltpu.make_async_remote_copy(
            src_ref=first_out,
            dst_ref=first_in.at[place],
            send_sem=fi_send.at[k - 1],
            recv_sem=fi_recv.at[k - 1],
            device_id={"tensor": lax.rem(me + k, count)},
            device_id_type=MESH,
        )

    def low_first():
        maps = down[...].reshape(3 * slots, width)
        for c in range(CHUNKS):
            part = dot_t(xg[rows(c), columns(me)], maps)
            mask = mask_ref[rows(c), :]
            for i in range(3):
                packed = pack(jnp.where(mask > 0, part[:, i * slots : (i + 1) * slots], 0.0))
                first_out[c, i] = packed
                first_in[me, c, i] = packed
        for k in range(1, count):
            first_copy(k, False).start()

    def low_part(c):
        lows = []
        for i in range(3):
            packed = first_in[0, c, i]
            for j in range(1, count):
                packed = packed + first_in[j, c, i]
            lows.append(unpack(packed, c))
        return lows

    def base_part(c):
        for h in range(0, query_cols, 2 * HEAD_WIDTH):
            base[:, h : h + 2 * HEAD_WIDTH] = dot(xg[rows(c), :], wq[:, h : h + 2 * HEAD_WIDTH])
        for i in range(2):
            start = query_cols + i * keyval_cols
            base[:, start : start + keyval_cols] = dot(xg[rows(c), :], wkv[i])

    def adapted(low, start, extent):
        return base[:, start : start + extent] + SCORE_SCALE * dot(
            low, small_rows(at_query + start, extent)
        )

    def rotary_part(c, lows):
        for h in range(0, query_cols, HEAD_WIDTH):
            piece = rotate(adapted(lows[0], h, HEAD_WIDTH), c)
            query[:, h : h + HEAD_WIDTH] = piece.astype(jnp.bfloat16)
        for h in range(0, keyval_cols, HEAD_WIDTH):
            piece = rotate(adapted(lows[1], at_key + h, HEAD_WIDTH), c)
            kv_ref[0, rows(c), h : h + HEAD_WIDTH] = piece.astype(jnp.bfloat16)
        kv_ref[1, rows(c), :] = adapted(lows[2], at_value, keyval_cols).astype(jnp.bfloat16)

    def attention_part(c, g):
        reach = (c + 1) * size
        t_index = c * size + lax.broadcasted_iota(jnp.int32, (size, reach), 0)
        s_index = lax.broadcasted_iota(jnp.int32, (size, reach), 1)
        allowed = jnp.logical_and(
            seg_ref[rows(c), :] == seg_row[:, :reach], s_index <= t_index
        )
        head = slice(g * HEAD_WIDTH, (g + 1) * HEAD_WIDTH)
        key = kv_ref[0, :reach, head]
        value = kv_ref[1, :reach, head]
        for i in range(group):
            spot = slice((g * group + i) * HEAD_WIDTH, (g * group + i + 1) * HEAD_WIDTH)
            scores = dot_t(query[:, spot], key) * HEAD_WIDTH ** (-0.5)
            scores = jnp.where(allowed, scores, NEG_FILL)
            grown = jnp.exp(scores - jnp.max(scores, axis=-1, keepdims=True))
            weights = (grown / jnp.sum(grown, axis=-1, keepdims=True)).astype(jnp.bfloat16)
            att[rows(c), spot] = dot(weights, value).astype(jnp.bfloat16)

    def reduce_copy(way, step, c):
        return pltpu.make_async_remote_copy(
            src_ref=rs_out.at[way, step - 1, c],
            dst_ref=rs_in.at[way, step - 1, c],
            send_sem=rs_send.at[way, step - 1, c],
            recv_sem=rs_recv.at[way, step - 1, c],
            device_id={"tensor": me + 1 if way == 0 else me - 1},
            device_id_type=MESH,
        )

    def sends_reduce(way, step):
        return me <= step - 1 if way == 0 else me >= count - step

    def has_before(way):
        return me >= 1 if way == 0 else me <= count - 2

    def reduce_step(c, step):
        for way in range(2):
            @pl.when(sends_reduce(way, step))
            def _():
                block = me + count - step if way == 0 else me - count + step
                acc[...] = dot(att[rows(c), :], wo[:, columns(block)])
                if step > 1:
                    @pl.when(has_before(way))
                    def _():
                        reduce_copy(way, step - 1, c).wait_recv()
                        acc[...] += rs_in[way, step - 2, c].astype(jnp.float32)
                rs_out[way, step - 1, c] = acc[...].astype(jnp.bfloat16)
                reduce_copy(way, step, c).start()

    def low_copy(k, c, receiving):
        place = lax.rem(me + count - k, count) if receiving else me
        return pltpu.make_async_remote_copy(
            src_ref=low_out.at[c],
            dst_ref=low_in.at[c, place],
            send_sem=lo_send.at[k - 1, c],
            recv_sem=lo_recv.at[k - 1, c],
            device_id={"tensor": lax.rem(me + k, count)},
            device_id_type=MESH,
        )

    def low_send(c):
        part = dot_t(att[rows(c), :], small_rows(at_down, query_cols))
        packed = pack(jnp.where(mask_ref[rows(c), :] > 0, part, 0.0))
        low_out[c] = packed
        low_in[c, me] = packed
        for k in range(1, count):
            low_copy(k, c, False).start()

    def finish(c):
        acc[...] = dot(att[rows(c), :], wo[:, columns(me)])
        for k in range(1, count):
            low_copy(k, c, True).wait_recv()
        packed = low_in[c, 0]
        for j in range(1, count):
            packed = packed + low_in[c, j]
        low = unpack(packed, c)
        acc[...] += SCORE_SCALE * dot(low, small_rows(at_up, width))
        for way in range(2):
            @pl.when(has_before(way))
            def _():
                reduce_copy(way, count - 1, c).wait_recv()
                acc[...] += rs_in[way, count - 2, c].astype(jnp.float32)
        mixed_ref[rows(c), :] = acc[...].astype(jnp.bfloat16)

    for copy in locals_[:3]:
        copy.wait()
    for hop in range(1, count):
        take_gather(0, hop)
    if CHUNKS > 2:
        send_gather(2, 1)
    for k in range(1, owners):
        adapter_copy(k, 0).wait_recv()
        adapter_copy(k, 1).wait_recv()
    low_first()
    for copy in locals_[3:]:
        copy.wait()
    take_gather(1, 1)
    base_part(0)
    for hop in range(2, count - 1):
        take_gather(1, hop)
    for k in range(1, count):
        first_copy(k, True).wait_recv()

    for c in range(CHUNKS):
        if c + 3 < CHUNKS:
            send_gather(c + 3, 1)
        work = [
            (lambda: base_part(c)) if c else (lambda: None),
            lambda: rotary_part(c, low_part(c)),
        ] + [functools.partial(attention_part, c, g) for g in range(keyval_cols // HEAD_WIDTH)]
        for i in range(max(len(work), count)):
            hop = i + 1
            if hop < count:
                if c >= 1:
                    reduce_step(c - 1, hop)
                if hop == 1 and c + 1 < CHUNKS:
                    take_gather(c + 1, count - 1)
                if hop > 1 and c + 2 < CHUNKS:
                    take_gather(c + 2, hop - 1)
            if i < len(work):
                work[i]()
        low_send(c)
        if c >= 2:
            finish(c - 2)
    for step in range(1, count):
        reduce_step(CHUNKS - 1, step)
        if step == 1:
            finish(CHUNKS - 2)
    finish(CHUNKS - 1)

    for k in range(1, count):
        first_copy(k, False).wait_send()
    for c in range(CHUNKS):
        for hop in range(1, count):
            for way in range(2):
                @pl.when(sends_gather(way, hop))
                def _():
                    gather_copy(way, hop, c, False).wait_send()

                @pl.when(sends_reduce(way, hop))
                def _():
                    reduce_copy(way, hop, c).wait_send()
            low_copy(hop, c, False).wait_send()
    for k in range(1, owners):
        adapter_copy(k, 0).wait_send()
        adapter_copy(k, 1).wait_send()


def local(
    normed_hidden,
    query_weight,
    key_value_weight,
    output_weight,
    adapter_down_rows,
    adapter_query_up,
    adapter_key_value_up,
    adapter_output_down,
    adapter_output_up,
    adapter_cache_row,
    request_adapter_index,
    request_token_length,
):
    token_count = normed_hidden.shape[0]
    slice_width = normed_hidden.shape[1]
    rank = adapter_query_up.shape[1]
    model_width = adapter_down_rows.shape[2]
    held_adapter_count = adapter_down_rows.shape[0]
    owners = lax.axis_size("adapter")
    count = lax.axis_size("tensor")
    query_cols = query_weight.shape[1]
    keyval_cols = key_value_weight.shape[2]
    size = token_count // CHUNKS

    request_ids = request_adapter_index[0]
    lengths = request_token_length[0]
    request_count = request_ids.shape[0]
    catalog = jnp.arange(adapter_cache_row.shape[0], dtype=jnp.int32)
    holder_rows = jnp.sum(
        jnp.where(request_ids[:, None] == catalog[None, :], adapter_cache_row[None, :], 0), axis=1
    )
    owner_index = holder_rows // held_adapter_count
    local_slot = holder_rows % held_adapter_count
    request_order = jnp.arange(request_count, dtype=jnp.int32)
    earlier = (owner_index[:, None] == owner_index[None, :]) & (
        request_order[None, :] < request_order[:, None]
    )
    rank_within = jnp.sum(earlier.astype(jnp.int32), axis=1)
    placed = owner_index * CAP + rank_within
    targets = jnp.arange(owners * CAP, dtype=jnp.int32)
    want_table = jnp.sum(
        jnp.where(placed[:, None] == targets[None, :], local_slot[:, None], 0), axis=0
    )
    picked = lax.all_to_all(
        want_table.reshape(owners, CAP), "adapter", split_axis=0, concat_axis=0, tiled=True
    )
    own_down = lax.dynamic_slice_in_dim(
        adapter_down_rows, lax.axis_index("tensor") * slice_width, slice_width, axis=2
    )
    down = jnp.take(own_down, picked, axis=0)
    down = down.reshape(owners, CAP, 3, rank, slice_width).transpose(0, 2, 1, 3, 4)
    down = down.reshape(owners, 3, CAP * rank, slice_width)
    small = jnp.concatenate(
        [
            jnp.take(adapter_query_up, picked, axis=0),
            jnp.take(adapter_key_value_up[:, 0], picked, axis=0),
            jnp.take(adapter_key_value_up[:, 1], picked, axis=0),
            jnp.take(adapter_output_down, picked, axis=0),
            jnp.take(adapter_output_up, picked, axis=0),
        ],
        axis=-1,
    )
    small_width = small.shape[-1]
    small = small.reshape(owners, CAP * rank, small_width)

    ending = jnp.cumsum(lengths)
    starting = ending - lengths
    token_index = jnp.arange(token_count, dtype=jnp.int32)
    segment = jnp.sum((token_index[:, None] >= ending[None, :]).astype(jnp.int32), axis=1)
    member = segment[:, None] == request_order[None, :]
    token_position = token_index - jnp.sum(jnp.where(member, starting[None, :], 0), axis=1)
    cosine, sine_part = rotation_tables(token_position)
    slot_of = jnp.sum(jnp.where(member, placed[None, :], 0), axis=1)
    slots = owners * CAP * rank
    mask = (slot_of[:, None] == (jnp.arange(slots, dtype=jnp.int32) // rank)[None, :]).astype(
        jnp.float32
    )

    any_spec = pl.BlockSpec(memory_space=pl.ANY)
    vmem = pl.BlockSpec(memory_space=pltpu.VMEM)
    packed = (size * rank // LANES, LANES)
    dma = pltpu.SemaphoreType.DMA
    mixed, kv_cache = pl.pallas_call(
        functools.partial(layer_kernel, count, owners, rank),
        out_shape=(
            jax.ShapeDtypeStruct((token_count, slice_width), jnp.bfloat16),
            jax.ShapeDtypeStruct((2, token_count, keyval_cols), jnp.bfloat16),
        ),
        in_specs=[any_spec] * 6 + [vmem] * 5,
        out_specs=(vmem, vmem),
        scratch_shapes=[
            pltpu.VMEM((token_count, model_width), jnp.bfloat16),
            pltpu.VMEM(query_weight.shape, jnp.bfloat16),
            pltpu.VMEM(key_value_weight.shape, jnp.bfloat16),
            pltpu.VMEM(output_weight.shape, jnp.bfloat16),
            pltpu.VMEM((3, owners, CAP * rank, slice_width), jnp.bfloat16),
            pltpu.VMEM((owners, CAP * rank, small_width), jnp.bfloat16),
            pltpu.VMEM((size, query_cols), jnp.bfloat16),
            pltpu.VMEM((size, query_cols + 2 * keyval_cols), jnp.float32),
            pltpu.VMEM((token_count, query_cols), jnp.bfloat16),
            pltpu.VMEM((size, slice_width), jnp.float32),
            pltpu.VMEM((2, count - 1, CHUNKS, size, slice_width), jnp.bfloat16),
            pltpu.VMEM((2, count - 1, CHUNKS, size, slice_width), jnp.bfloat16),
            pltpu.VMEM((CHUNKS,) + packed, jnp.float32),
            pltpu.VMEM((CHUNKS, count) + packed, jnp.float32),
            pltpu.VMEM((CHUNKS, 3) + packed, jnp.float32),
            pltpu.VMEM((count, CHUNKS, 3) + packed, jnp.float32),
            dma((2, count - 1, CHUNKS)),
            dma((2, count - 1, CHUNKS)),
            dma((2, count - 1, CHUNKS)),
            dma((2, count - 1, CHUNKS)),
            dma((count - 1, CHUNKS)),
            dma((count - 1, CHUNKS)),
            dma((count - 1,)),
            dma((count - 1,)),
            dma((owners - 1, 2)),
            dma((owners - 1, 2)),
            dma((6,)),
        ],
        compiler_params=pltpu.CompilerParams(
            collective_id=0, has_side_effects=True, vmem_limit_bytes=60 * 1024 * 1024
        ),
    )(
        normed_hidden, query_weight, key_value_weight, output_weight, down, small,
        cosine, sine_part, mask, segment[:, None], segment[None, :],
    )
    return (mixed, kv_cache)


def solution(mesh):
    in_specs = (
        P(("groups", "adapter"), "tensor"),
        P(None, "tensor"),
        P(None, None, "tensor"),
        P("tensor", None),
        P(("groups", "adapter"), None, None),
        P(("groups", "adapter"), None, "tensor"),
        P(("groups", "adapter"), None, None, "tensor"),
        P(("groups", "adapter"), None, "tensor"),
        P(("groups", "adapter"), None, "tensor"),
        P("groups"),
        P(("groups", "adapter"), None),
        P(("groups", "adapter"), None),
    )
    out_specs = (P(("groups", "adapter"), "tensor"), P(None, ("groups", "adapter"), "tensor"))
    return jax.shard_map(local, mesh=mesh, in_specs=in_specs, out_specs=out_specs, check_vma=False)
```
